512 devices in a mesh: dp: 8 (over y_lo, core), ctx: 64 (over z, y_hi, x).
Axes of the slice: x: 4, y: 8 (y_hi: 2, y_lo: 4; y = y_hi * 4 + y_lo), z: 8, core: 2. Of those that a mesh axis runs over, the one named last changes fastest.
Arguments:
- query_rows: bfloat16 [512, 256, 2048], P(('dp', 'ctx')), parts along dimension 0, may hold values from -32 to 32
- key_rows: bfloat16 [512, 256, 2048], P(('dp', 'ctx')), parts along dimension 0, may hold values from -32 to 32
- value_rows: bfloat16 [512, 256, 2048], P(('dp', 'ctx')), parts along dimension 0, may hold values from -6 to 6
Outputs:
- temporal_out: bfloat16 [512, 256, 2048], P(('dp', 'ctx')), parts along dimension 0
The draws below stay inside these ranges and needn't reach their ends.
There are 8 independent parts, one for each index of `dp`. The reference program is written for one: setup_inputs(seed, part) draws one part's arguments, and reference() takes and returns one part's arrays. A program takes and returns all parts, laid end to end along the dimension named above; each array names one. Nothing has to cross between parts.
All inputs are finite; a program needn't handle non-finite values.
Results may differ from the reference program's by a relative error of at most 0.0064.
Values may be sent and summed in bfloat16 or wider, within the bound.
A program may use at most 64 MiB of HBM per device.

```python
import jax
import jax.numpy as jnp
from jax import lax

HEADS = 16
HD = 128
TOK = 256
FRAMES = 64


def draw_query_rows(key, part):
    key = jax.random.fold_in(key, 11)
    shape = (FRAMES, TOK, HEADS * HD)
    result = jnp.clip(1.5 * jax.random.normal(key, shape, jnp.float32), -9.0, 9.0)
    return jnp.clip(result, -32.0, 32.0).astype(jnp.bfloat16)


def draw_key_rows(key, part):
    key = jax.random.fold_in(key, 23)
    shape = (FRAMES, TOK, HEADS * HD)
    result = jnp.clip(1.5 * jax.random.normal(key, shape, jnp.float32), -9.0, 9.0)
    return jnp.clip(result, -32.0, 32.0).astype(jnp.bfloat16)


def level_of(rng, dims, shards, smallest, top_value):
    level = 1.0
    for axis_at, shards_of in shards:
        draws = jax.random.uniform(jax.random.fold_in(jax.random.fold_in(rng, 6), axis_at), (shards_of,), jnp.float32, smallest / len(shards), top_value / len(shards))
        level = level * jnp.repeat(jnp.exp(draws), dims[axis_at] // shards_of).reshape((-1,) + (1,) * (len(dims) - 1 - axis_at))
    return level


def noise(rng, extent, deviation, most, shards=(), kind=jnp.bfloat16):
    array = deviation * jax.random.normal(rng, extent, jnp.float32)
    if shards:
        array = array * level_of(rng, extent, shards, -0.22, 0.18)
    return jnp.clip(array, -most, most).astype(kind)


def setup_inputs(seed: int = 0, part: int = 0) -> dict:
    keys = jax.random.split(jax.random.key(seed), 4)
    part_keys = jax.random.split(jax.random.fold_in(keys[3], part), 4)
    query_rows = draw_query_rows(jax.random.fold_in(jax.random.fold_in(keys[3], part), 71), part)
    key_rows = draw_key_rows(jax.random.fold_in(jax.random.fold_in(keys[3], part), 71), part)
    value_rows = noise(part_keys[2], (FRAMES, TOK, HEADS * HD), 1.0, 6.0, ((0, 64),))
    return {"query_rows": query_rows, "key_rows": key_rows, "value_rows": value_rows}


def spatial_frame(query_frame, key_frame, value_frame):
    inv_root = HD ** -0.5
    shaped_q = query_frame.reshape(TOK, HEADS, HD).astype(jnp.float32)
    shaped_k = key_frame.reshape(TOK, HEADS, HD).astype(jnp.float32)
    shaped_v = value_frame.reshape(TOK, HEADS, HD).astype(jnp.float32)
    scores = jnp.einsum("thd,shd->hts", shaped_q, shaped_k) * inv_root
    weights = jax.nn.softmax(scores, axis=-1).astype(jnp.bfloat16)
    weights = lax.optimization_barrier(weights).astype(jnp.float32)
    result = jnp.einsum("hts,shd->thd", weights, shaped_v)
    return result.reshape(TOK, HEADS * HD).astype(jnp.bfloat16)


def reference(query_rows, key_rows, value_rows):
    inv_root = HD ** -0.5
    spatial_out = lax.map(lambda trio: spatial_frame(trio[0], trio[1], trio[2]), (query_rows, key_rows, value_rows))
    shaped_q = query_rows.reshape(FRAMES, TOK, HEADS, HD).astype(jnp.float32)
    shaped_k = key_rows.reshape(FRAMES, TOK, HEADS, HD).astype(jnp.float32)
    shaped_v = spatial_out.reshape(FRAMES, TOK, HEADS, HD).astype(jnp.float32)
    scores = jnp.einsum("fthd,gthd->thfg", shaped_q, shaped_k) * inv_root
    weights = jax.nn.softmax(scores, axis=-1).astype(jnp.bfloat16)
    weights = lax.optimization_barrier(weights).astype(jnp.float32)
    result = jnp.einsum("thfg,gthd->fthd", weights, shaped_v)
    return result.reshape(FRAMES, TOK, HEADS * HD).astype(jnp.bfloat16)
```

```python
import functools
import math

import jax
import jax.numpy as jnp
from jax import lax
from jax.experimental import pallas as pl
from jax.experimental.pallas import tpu as pltpu
from jax.sharding import PartitionSpec as P

HEADS = 16
HD = 128
TOK = 256
FRAMES = 64
WIDTH = HEADS * HD
SLOTS = 4
CHUNKS = HEADS // SLOTS
PLACES = 16
MESH = pl.DeviceIdType.MESH
SCALE = HD**-0.5 * math.log2(math.e)
STRIDE = 27


def attend(q, k, v, keep=None):
    scores = lax.dot_general(q, k, (((1,), (1,)), ((), ())), preferred_element_type=jnp.float32)
    if keep is not None:
        scores = jnp.where(keep, scores, -jnp.inf)
    top = jnp.max(scores, axis=1, keepdims=True)
    weights = jnp.exp2((scores - top) * SCALE)
    total = jnp.sum(weights, axis=1, keepdims=True)
    weights = (weights * (1.0 / total)).astype(jnp.bfloat16)
    return jnp.dot(weights, v, preferred_element_type=jnp.float32)


def kernel(q_hbm, k_hbm, v_hbm, o_hbm, qk, v, mid, r_qk, r_v, turned, back, o_part, out, load, s_qk, s_v, s_o, g_qk, g_v, g_o, store):
    clip, me = lax.axis_index("dp"), lax.axis_index("ctx")
    loads = [
        pltpu.make_async_copy(q_hbm, qk.at[0], load.at[0]),
        pltpu.make_async_copy(k_hbm, qk.at[1], load.at[1]),
        pltpu.make_async_copy(v_hbm, v, load.at[2]),
    ]
    for copy in loads:
        copy.start()

    def at(peer):
        return {"dp": clip, "ctx": peer}

    def peer_of(i):
        r = lax.rem(i * STRIDE, FRAMES)
        x = lax.rem(lax.rem(me, 4) + lax.rem(r, 4), 4)
        y = lax.rem(lax.rem(me // 4, 2) + lax.rem(r // 4, 2), 2)
        z = lax.rem(me // 8 + r // 8, 8)
        return (z * 2 + y) * 4 + x

    barrier = pltpu.get_barrier_semaphore()

    @pl.loop(1, FRAMES)
    def _(i):
        pl.semaphore_signal(barrier, inc=1, device_id=at(peer_of(i)), device_id_type=MESH)

    pl.semaphore_wait(barrier, FRAMES - 1)

    def block(chunk, peer):
        rows = pl.ds(pl.multiple_of((peer // SLOTS) * PLACES, PLACES), PLACES)
        cols = pl.ds(pl.multiple_of((chunk * SLOTS + lax.rem(peer, SLOTS)) * HD, HD), HD)
        return rows, cols

    def send_qk(chunk):
        rows, cols = block(chunk, me)
        pltpu.make_async_copy(qk.at[:, rows, cols], r_qk.at[chunk, :, me], g_qk.at[chunk]).start()

        @pl.loop(1, FRAMES)
        def _(i):
            peer = peer_of(i)
            rows, cols = block(chunk, peer)
            pltpu.make_async_remote_copy(
                src_ref=qk.at[:, rows, cols], dst_ref=r_qk.at[chunk, :, me],
                send_sem=s_qk.at[chunk], recv_sem=g_qk.at[chunk],
                device_id=at(peer), device_id_type=MESH,
            ).start()

    def send_mid(chunk):
        rows, cols = block(chunk, me)
        pltpu.make_async_copy(mid.at[rows, cols], r_v.at[chunk, me], g_v.at[chunk]).start()

        @pl.loop(1, FRAMES)
        def _(i):
            peer = peer_of(i)
            rows, cols = block(chunk, peer)
            pltpu.make_async_remote_copy(
                src_ref=mid.at[rows, cols], dst_ref=r_v.at[chunk, me],
                send_sem=s_v.at[chunk], recv_sem=g_v.at[chunk],
                device_id=at(peer), device_id_type=MESH,
            ).start()

    def send_back(chunk):
        rows, cols = block(chunk, me)
        pltpu.make_async_copy(o_part.at[chunk, me], out.at[rows, cols], g_o.at[chunk]).start()

        @pl.loop(1, FRAMES)
        def _(i):
            peer = peer_of(i)
            pltpu.make_async_remote_copy(
                src_ref=o_part.at[chunk, peer], dst_ref=out.at[rows, cols],
                send_sem=s_o.at[chunk], recv_sem=g_o.at[chunk],
                device_id=at(peer), device_id_type=MESH,
            ).start()

    def arrived(ref, sem):
        pltpu.make_async_copy(ref, ref, sem).wait()

    def spatial(chunk):
        @pl.loop(0, SLOTS)
        def _(slot):
            cols = pl.ds(pl.multiple_of((chunk * SLOTS + slot) * HD, HD), HD)
            mid[:, cols] = attend(qk[0, :, cols], qk[1, :, cols], v[:, cols]).astype(jnp.bfloat16)

    side = lax.broadcasted_iota(jnp.int32, (2 * FRAMES, 2 * FRAMES), 0) // FRAMES
    other = lax.broadcasted_iota(jnp.int32, (2 * FRAMES, 2 * FRAMES), 1) // FRAMES
    keep = side == other

    def temporal(chunk):
        turned[0] = r_qk[chunk, 0].reshape(FRAMES * PLACES, HD).astype(jnp.float32)
        turned[1] = r_qk[chunk, 1].reshape(FRAMES * PLACES, HD).astype(jnp.float32)
        turned[2] = r_v[chunk].reshape(FRAMES * PLACES, HD).astype(jnp.float32)
        for t in range(0, PLACES, 2):
            trio = [
                jnp.concatenate(
                    [turned[a, pl.ds(t + s, FRAMES, stride=PLACES), :] for s in range(2)], axis=0
                ).astype(jnp.bfloat16)
                for a in range(3)
            ]
            both = attend(*trio, keep)
            back[pl.ds(t, FRAMES, stride=PLACES), :] = both[:FRAMES]
            back[pl.ds(t + 1, FRAMES, stride=PLACES), :] = both[FRAMES:]
        o_part[chunk] = back[...].astype(jnp.bfloat16).reshape(FRAMES, PLACES, HD)

    loads[0].wait()
    loads[1].wait()

    @pl.loop(0, CHUNKS)
    def _(chunk):
        send_qk(chunk)

    loads[2].wait()

    @pl.loop(0, CHUNKS)
    def _(chunk):
        spatial(chunk)
        send_mid(chunk)

    @pl.loop(0, CHUNKS)
    def _(chunk):
        arrived(r_qk.at[chunk], g_qk.at[chunk])
        arrived(r_v.at[chunk], g_v.at[chunk])
        temporal(chunk)
        send_back(chunk)

    def result(chunk):
        cols = pl.ds(pl.multiple_of(chunk * SLOTS * HD, SLOTS * HD), SLOTS * HD)
        return pltpu.make_async_copy(out.at[:, cols], o_hbm.at[:, cols], store.at[chunk])

    for chunk in range(CHUNKS):
        cols = pl.ds(chunk * SLOTS * HD, SLOTS * HD)
        arrived(out.at[:, cols], g_o.at[chunk])
        result(chunk).start()
    for chunk in range(CHUNKS):
        sent = pl.ds(0, FRAMES - 1)
        arrived(r_qk.at[chunk, :, sent], s_qk.at[chunk])
        arrived(r_v.at[chunk, sent], s_v.at[chunk])
        arrived(o_part.at[chunk, sent], s_o.at[chunk])
        result(chunk).wait()


def local(query_rows, key_rows, value_rows):
    shape = query_rows.shape
    rows = (TOK, WIDTH)
    anywhere = pl.BlockSpec(memory_space=pl.ANY)
    sem = pltpu.SemaphoreType.DMA
    result = pl.pallas_call(
        kernel,
        out_shape=jax.ShapeDtypeStruct(rows, jnp.bfloat16),
        in_specs=[anywhere] * 3,
        out_specs=anywhere,
        scratch_shapes=[
            pltpu.VMEM((2,) + rows, jnp.bfloat16),
            pltpu.VMEM(rows, jnp.bfloat16),
            pltpu.VMEM(rows, jnp.bfloat16),
            pltpu.VMEM((CHUNKS, 2, FRAMES, PLACES, HD), jnp.bfloat16),
            pltpu.VMEM((CHUNKS, FRAMES, PLACES, HD), jnp.bfloat16),
            pltpu.VMEM((3, FRAMES * PLACES, HD), jnp.float32),
            pltpu.VMEM((FRAMES * PLACES, HD), jnp.float32),
            pltpu.VMEM((CHUNKS, FRAMES, PLACES, HD), jnp.bfloat16),
            pltpu.VMEM(rows, jnp.bfloat16),
            sem((3,)),
        ]
        + [sem((CHUNKS,))] * 7,
        compiler_params=pltpu.CompilerParams(
            collective_id=0, has_side_effects=True, vmem_limit_bytes=48 * 1024 * 1024
        ),
        name="two_cores",
    )(query_rows.reshape(rows), key_rows.reshape(rows), value_rows.reshape(rows))
    return result.reshape(shape)


def solution(mesh):
    spec = P(("dp", "ctx"), None, None)
    return jax.shard_map(local, mesh=mesh, in_specs=(spec,) * 3, out_specs=spec, check_vma=False)
```

```python
import functools
import math

import jax
import jax.numpy as jnp
from jax import lax
from jax.experimental import pallas as pl
from jax.experimental.pallas import tpu as pltpu
from jax.sharding import PartitionSpec as P

HEADS = 16
HD = 128
TOK = 256
FRAMES = 64
WIDTH = HEADS * HD
SLOTS = 4
CHUNKS = HEADS // SLOTS
PLACES = 16
MESH = pl.DeviceIdType.MESH
SCALE = HD**-0.5 * math.log2(math.e)
LINE = 8
FLAT = 8
STRIDE = 37
REST_STRIDE = 18
FAR_FIRST = sorted(
    range(1, FRAMES),
    key=lambda r: -(min(r // 8, 8 - r // 8) + 4 * (r // 4 % 2) + 0.5 * min(r % 4, 4 - r % 4)),
)


def attend(q, k, v, keep=None):
    scores = lax.dot_general(q, k, (((1,), (1,)), ((), ())), preferred_element_type=jnp.float32)
    if keep is not None:
        scores = jnp.where(keep, scores, -jnp.inf)
    top = jnp.max(scores, axis=1, keepdims=True)
    weights = jnp.exp2((scores - top) * SCALE)
    total = jnp.sum(weights, axis=1, keepdims=True)
    weights = (weights * (1.0 / total)).astype(jnp.bfloat16)
    return jnp.dot(weights, v, preferred_element_type=jnp.float32)


def kernel(q_hbm, k_hbm, v_hbm, o_hbm, qk, v, mid, r_qk, r_v, turned, back, o_part, ready, load, s_qk, s_v, s_o, g_qk, g_v, g_o):
    clip, me = lax.axis_index("dp"), lax.axis_index("ctx")
    loads = [
        pltpu.make_async_copy(q_hbm, qk.at[0], load.at[0]),
        pltpu.make_async_copy(k_hbm, qk.at[1], load.at[1]),
        pltpu.make_async_copy(v_hbm, v, load.at[2]),
    ]
    for copy in loads:
        copy.start()

    def at(peer):
        return {"dp": clip, "ctx": peer}

    x, y, z = lax.rem(me, 4), lax.rem(me // 4, 2), me // 8

    def moved(flat, line):
        new_x, new_y = lax.rem(x + lax.rem(flat, 4), 4), lax.rem(y + flat // 4, 2)
        return (lax.rem(z + line, LINE) * 2 + new_y) * 4 + new_x

    def every(i):
        r = lax.rem(i * STRIDE, FRAMES)
        return moved(lax.rem(r, FLAT), r // FLAT)

    def rest(i):
        r = lax.rem(i * REST_STRIDE, (FLAT - 1) * (LINE - 1))
        return moved(r // (LINE - 1) + 1, lax.rem(r, LINE - 1) + 1)

    barrier = pltpu.get_barrier_semaphore()
    for i in range(1, LINE):
        pl.semaphore_signal(barrier, inc=1, device_id=at(moved(0, i)), device_id_type=MESH)
    for i in range(1, FLAT):
        pl.semaphore_signal(barrier, inc=1, device_id=at(moved(i, 0)), device_id_type=MESH)
    pl.semaphore_wait(barrier, LINE + FLAT - 2)
    for i in range(1, FLAT):
        pl.semaphore_signal(ready, inc=1, device_id=at(moved(i, 0)), device_id_type=MESH)

    def block(chunk, peer):
        rows = pl.ds(pl.multiple_of((peer // SLOTS) * PLACES, PLACES), PLACES)
        cols = pl.ds(pl.multiple_of((chunk * SLOTS + lax.rem(peer, SLOTS)) * HD, HD), HD)
        return rows, cols

    def send_qk(chunk, peer):
        rows, cols = block(chunk, peer)
        pltpu.make_async_remote_copy(
            src_ref=qk.at[:, rows, cols], dst_ref=r_qk.at[chunk, :, me],
            send_sem=s_qk.at[chunk], recv_sem=g_qk.at[chunk],
            device_id=at(peer), device_id_type=MESH,
        ).start()

    def send_qk_near(chunk):
        rows, cols = block(chunk, me)
        pltpu.make_async_copy(qk.at[:, rows, cols], r_qk.at[chunk, :, me], g_qk.at[chunk]).start()

        @pl.loop(1, LINE)
        def _(i):
            send_qk(chunk, moved(i, 0))
            send_qk(chunk, moved(0, i))

    def send_qk_rest(chunk):
        @pl.loop(0, (FLAT - 1) * (LINE - 1))
        def _(i):
            send_qk(chunk, rest(i))

    def send_mid(chunk):
        rows, cols = block(chunk, me)
        pltpu.make_async_copy(mid.at[rows, cols], r_v.at[chunk, me], g_v.at[chunk]).start()

        @pl.loop(1, FRAMES)
        def _(i):
            peer = every(i)
            rows, cols = block(chunk, peer)
            pltpu.make_async_remote_copy(
                src_ref=mid.at[rows, cols], dst_ref=r_v.at[chunk, me],
                send_sem=s_v.at[chunk], recv_sem=g_v.at[chunk],
                device_id=at(peer), device_id_type=MESH,
            ).start()

    def send_back(chunk):
        rows, cols = block(chunk, me)
        pltpu.make_async_copy(o_part.at[chunk, me], o_hbm.at[rows, cols], g_o.at[chunk]).start()

        for r in FAR_FIRST:
            peer = moved(r % FLAT, r // FLAT)
            pltpu.make_async_remote_copy(
                src_ref=o_part.at[chunk, peer], dst_ref=o_hbm.at[rows, cols],
                send_sem=s_o.at[chunk], recv_sem=g_o.at[chunk],
                device_id=at(peer), device_id_type=MESH,
            ).start()

    def arrived(ref, sem):
        pltpu.make_async_copy(ref, ref, sem).wait()

    def spatial(chunk):
        @pl.loop(0, SLOTS)
        def _(slot):
            cols = pl.ds(pl.multiple_of((chunk * SLOTS + slot) * HD, HD), HD)
            mid[:, cols] = attend(qk[0, :, cols], qk[1, :, cols], v[:, cols]).astype(jnp.bfloat16)

    side = lax.broadcasted_iota(jnp.int32, (2 * FRAMES, 2 * FRAMES), 0) // FRAMES
    other = lax.broadcasted_iota(jnp.int32, (2 * FRAMES, 2 * FRAMES), 1) // FRAMES
    keep = side == other

    def temporal(chunk):
        turned[0] = r_qk[chunk, 0].reshape(FRAMES * PLACES, HD).astype(jnp.float32)
        turned[1] = r_qk[chunk, 1].reshape(FRAMES * PLACES, HD).astype(jnp.float32)
        turned[2] = r_v[chunk].reshape(FRAMES * PLACES, HD).astype(jnp.float32)
        for t in range(0, PLACES, 2):
            trio = [
                jnp.concatenate(
                    [turned[a, pl.ds(t + s, FRAMES, stride=PLACES), :] for s in range(2)], axis=0
                ).astype(jnp.bfloat16)
                for a in range(3)
            ]
            both = attend(*trio, keep)
            back[pl.ds(t, FRAMES, stride=PLACES), :] = both[:FRAMES]
            back[pl.ds(t + 1, FRAMES, stride=PLACES), :] = both[FRAMES:]
        o_part[chunk] = back[...].astype(jnp.bfloat16).reshape(FRAMES, PLACES, HD)

    loads[0].wait()
    loads[1].wait()

    @pl.loop(0, CHUNKS)
    def _(chunk):
        send_qk_near(chunk)

    pl.semaphore_wait(ready, FLAT - 1)

    @pl.loop(0, CHUNKS)
    def _(chunk):
        send_qk_rest(chunk)

    loads[2].wait()

    @pl.loop(0, CHUNKS)
    def _(chunk):
        spatial(chunk)
        send_mid(chunk)

    @pl.loop(0, CHUNKS)
    def _(chunk):
        arrived(r_qk.at[chunk], g_qk.at[chunk])
        arrived(r_v.at[chunk], g_v.at[chunk])
        temporal(chunk)
        send_back(chunk)

    for chunk in range(CHUNKS):
        cols = pl.ds(chunk * SLOTS * HD, SLOTS * HD)
        arrived(o_hbm.at[:, cols], g_o.at[chunk])
    for chunk in range(CHUNKS):
        sent = pl.ds(0, FRAMES - 1)
        arrived(r_qk.at[chunk, :, sent], s_qk.at[chunk])
        arrived(r_v.at[chunk, sent], s_v.at[chunk])
        arrived(o_part.at[chunk, sent], s_o.at[chunk])


def local(query_rows, key_rows, value_rows):
    shape = query_rows.shape
    rows = (TOK, WIDTH)
    anywhere = pl.BlockSpec(memory_space=pl.ANY)
    sem = pltpu.SemaphoreType.DMA
    result = pl.pallas_call(
        kernel,
        out_shape=jax.ShapeDtypeStruct(rows, jnp.bfloat16),
        in_specs=[anywhere] * 3,
        out_specs=anywhere,
        scratch_shapes=[
            pltpu.VMEM((2,) + rows, jnp.bfloat16),
            pltpu.VMEM(rows, jnp.bfloat16),
            pltpu.VMEM(rows, jnp.bfloat16),
            pltpu.VMEM((CHUNKS, 2, FRAMES, PLACES, HD), jnp.bfloat16),
            pltpu.VMEM((CHUNKS, FRAMES, PLACES, HD), jnp.bfloat16),
            pltpu.VMEM((3, FRAMES * PLACES, HD), jnp.float32),
            pltpu.VMEM((FRAMES * PLACES, HD), jnp.float32),
            pltpu.VMEM((CHUNKS, FRAMES, PLACES, HD), jnp.bfloat16),
            pltpu.SemaphoreType.REGULAR,
            sem((3,)),
        ]
        + [sem((CHUNKS,))] * 6,
        compiler_params=pltpu.CompilerParams(
            collective_id=0, has_side_effects=True, vmem_limit_bytes=63 * 1024 * 1024
        ),
        name="two_cores",
    )(query_rows.reshape(rows), key_rows.reshape(rows), value_rows.reshape(rows))
    return result.reshape(shape)


def solution(mesh):
    spec = P(("dp", "ctx"), None, None)
    return jax.shard_map(local, mesh=mesh, in_specs=(spec,) * 3, out_specs=spec, check_vma=False)
```

```python
import functools
import math

import jax
import jax.numpy as jnp
from jax import lax
from jax.experimental import pallas as pl
from jax.experimental.pallas import tpu as pltpu
from jax.sharding import PartitionSpec as P

HEADS = 16
HD = 128
TOK = 256
FRAMES = 64
WIDTH = HEADS * HD
SLOTS = 4
CHUNKS = HEADS // SLOTS
PLACES = 16
MESH = pl.DeviceIdType.MESH
SCALE = HD**-0.5 * math.log2(math.e)
LINE = 8
FLAT = 8
STRIDE = 37
GROUPS = ((1, 4), (3, 5), (2, 7, 6))
LINES = ((4, 3, 5, 2, 6, 1, 7), (1, 7, 2, 6, 3, 5, 4), (3, 5, 1, 7, 4, 2, 6))
FAR_FIRST = sorted(
    range(1, FRAMES),
    key=lambda r: -(min(r // 8, 8 - r // 8) + 4 * (r // 4 % 2) + 0.5 * min(r % 4, 4 - r % 4)),
)


def attend(q, k, v, keep=None):
    scores = lax.dot_general(q, k, (((1,), (1,)), ((), ())), preferred_element_type=jnp.float32)
    if keep is not None:
        scores = jnp.where(keep, scores, -jnp.inf)
    top = jnp.max(scores, axis=1, keepdims=True)
    weights = jnp.exp2((scores - top) * SCALE)
    total = jnp.sum(weights, axis=1, keepdims=True)
    weights = (weights * (1.0 / total)).astype(jnp.bfloat16)
    return jnp.dot(weights, v, preferred_element_type=jnp.float32)


def kernel(q_hbm, k_hbm, v_hbm, o_hbm, qk, v, mid, r_qk, r_v, turned, back, o_part, ready, load, s_qk, s_v, s_o, g_qk, g_v, g_o):
    clip, me = lax.axis_index("dp"), lax.axis_index("ctx")
    loads = [
        pltpu.make_async_copy(q_hbm, qk.at[0], load.at[0]),
        pltpu.make_async_copy(k_hbm, qk.at[1], load.at[1]),
        pltpu.make_async_copy(v_hbm, v, load.at[2]),
    ]
    for copy in loads:
        copy.start()

    def at(peer):
        return {"dp": clip, "ctx": peer}

    x, y, z = lax.rem(me, 4), lax.rem(me // 4, 2), me // 8
    turn_x, turn_z = 1 + 2 * lax.rem(clip, 2), 1 + 6 * lax.rem(clip, 2)

    def moved(flat, line):
        new_x = lax.rem(x + lax.rem(flat, 4) * turn_x, 4)
        new_y = lax.rem(y + flat // 4, 2)
        return (lax.rem(z + line * turn_z, LINE) * 2 + new_y) * 4 + new_x

    def every(i):
        r = lax.rem(i * STRIDE, FRAMES)
        return moved(lax.rem(r, FLAT), r // FLAT)

    barrier = pltpu.get_barrier_semaphore()
    for i in range(1, LINE):
        pl.semaphore_signal(barrier, inc=1, device_id=at(moved(0, i)), device_id_type=MESH)
    for i in range(1, FLAT):
        pl.semaphore_signal(barrier, inc=1, device_id=at(moved(i, 0)), device_id_type=MESH)
    pl.semaphore_wait(barrier, LINE + FLAT - 2)
    for i in reversed(range(1, FLAT)):
        back_to_me = (FLAT + 4 - i if i > 4 else 4 - i if i < 4 else 4)
        pl.semaphore_signal(ready.at[back_to_me], inc=1, device_id=at(moved(i, 0)), device_id_type=MESH)

    def block(chunk, peer):
        rows = pl.ds(pl.multiple_of((peer // SLOTS) * PLACES, PLACES), PLACES)
        cols = pl.ds(pl.multiple_of((chunk * SLOTS + lax.rem(peer, SLOTS)) * HD, HD), HD)
        return rows, cols

    def send_qk(chunk, peer):
        rows, cols = block(chunk, peer)
        pltpu.make_async_remote_copy(
            src_ref=qk.at[:, rows, cols], dst_ref=r_qk.at[chunk, :, me],
            send_sem=s_qk.at[chunk], recv_sem=g_qk.at[chunk],
            device_id=at(peer), device_id_type=MESH,
        ).start()

    def send_qk_near(chunk):
        rows, cols = block(chunk, me)
        pltpu.make_async_copy(qk.at[:, rows, cols], r_qk.at[chunk, :, me], g_qk.at[chunk]).start()

        @pl.loop(1, LINE)
        def _(i):
            send_qk(chunk, moved(i, 0))
            send_qk(chunk, moved(0, i))

    def send_qk_lines(flats):
        for flat in flats:
            pl.semaphore_wait(ready.at[flat], 1)

        @pl.loop(0, CHUNKS)
        def _(chunk):
            for i in range(LINE - 1):
                for flat, lines in zip(flats, LINES):
                    send_qk(chunk, moved(flat, lines[i]))

    def send_mid(chunk):
        rows, cols = block(chunk, me)
        pltpu.make_async_copy(mid.at[rows, cols], r_v.at[chunk, me], g_v.at[chunk]).start()

        @pl.loop(1, FRAMES)
        def _(i):
            peer = every(i)
            rows, cols = block(chunk, peer)
            pltpu.make_async_remote_copy(
                src_ref=mid.at[rows, cols], dst_ref=r_v.at[chunk, me],
                send_sem=s_v.at[chunk], recv_sem=g_v.at[chunk],
                device_id=at(peer), device_id_type=MESH,
            ).start()

    def keep_back(chunk):
        rows, cols = block(chunk, me)
        pltpu.make_async_copy(o_part.at[chunk, me], o_hbm.at[rows, cols], g_o.at[chunk]).start()

    def send_back(chunk, low, high):
        rows, cols = block(chunk, me)
        for r in FAR_FIRST:
            peer = moved(r % FLAT, r // FLAT)

            @pl.when(jnp.logical_and(peer >= low * FLAT, peer < high * FLAT))
            def _():
                pltpu.make_async_remote_copy(
                    src_ref=o_part.at[chunk, peer], dst_ref=o_hbm.at[rows, cols],
                    send_sem=s_o.at[chunk], recv_sem=g_o.at[chunk],
                    device_id=at(peer), device_id_type=MESH,
                ).start()

    def arrived(ref, sem):
        pltpu.make_async_copy(ref, ref, sem).wait()

    def spatial(chunk):
        @pl.loop(0, SLOTS)
        def _(slot):
            cols = pl.ds(pl.multiple_of((chunk * SLOTS + slot) * HD, HD), HD)
            mid[:, cols] = attend(qk[0, :, cols], qk[1, :, cols], v[:, cols]).astype(jnp.bfloat16)

    side = lax.broadcasted_iota(jnp.int32, (2 * FRAMES, 2 * FRAMES), 0) // FRAMES
    other = lax.broadcasted_iota(jnp.int32, (2 * FRAMES, 2 * FRAMES), 1) // FRAMES
    keep = side == other

    def temporal(chunk):
        turned[0] = r_qk[chunk, 0].reshape(FRAMES * PLACES, HD).astype(jnp.float32)
        turned[1] = r_qk[chunk, 1].reshape(FRAMES * PLACES, HD).astype(jnp.float32)
        turned[2] = r_v[chunk].reshape(FRAMES * PLACES, HD).astype(jnp.float32)
        for t in range(0, PLACES, 2):
            trio = [
                jnp.concatenate(
                    [turned[a, pl.ds(t + s, FRAMES, stride=PLACES), :] for s in range(2)], axis=0
                ).astype(jnp.bfloat16)
                for a in range(3)
            ]
            both = attend(*trio, keep)
            back[pl.ds(t, FRAMES, stride=PLACES), :] = both[:FRAMES]
            back[pl.ds(t + 1, FRAMES, stride=PLACES), :] = both[FRAMES:]
        o_part[chunk] = back[...].astype(jnp.bfloat16).reshape(FRAMES, PLACES, HD)

    loads[0].wait()
    loads[1].wait()

    @pl.loop(0, CHUNKS)
    def _(chunk):
        send_qk_near(chunk)

    for flats in GROUPS:
        send_qk_lines(flats)

    loads[2].wait()

    @pl.loop(0, CHUNKS)
    def _(chunk):
        spatial(chunk)
        send_mid(chunk)

    @pl.loop(0, CHUNKS)
    def _(chunk):
        arrived(r_qk.at[chunk], g_qk.at[chunk])
        arrived(r_v.at[chunk], g_v.at[chunk])
        temporal(chunk)
        keep_back(chunk)

        @pl.when(chunk < CHUNKS - 2)
        def _():
            send_back(chunk, 0, LINE)

        @pl.when(chunk >= CHUNKS - 2)
        def _():
            send_back(chunk, 0, 2)

    for chunk in (CHUNKS - 2, CHUNKS - 1):
        send_back(chunk, 2, LINE)

    for chunk in range(CHUNKS):
        cols = pl.ds(chunk * SLOTS * HD, SLOTS * HD)
        arrived(o_hbm.at[:, cols], g_o.at[chunk])
    for chunk in range(CHUNKS):
        sent = pl.ds(0, FRAMES - 1)
        arrived(r_qk.at[chunk, :, sent], s_qk.at[chunk])
        arrived(r_v.at[chunk, sent], s_v.at[chunk])
        arrived(o_part.at[chunk, sent], s_o.at[chunk])


def local(query_rows, key_rows, value_rows):
    shape = query_rows.shape
    rows = (TOK, WIDTH)
    anywhere = pl.BlockSpec(memory_space=pl.ANY)
    sem = pltpu.SemaphoreType.DMA
    result = pl.pallas_call(
        kernel,
        out_shape=jax.ShapeDtypeStruct(rows, jnp.bfloat16),
        in_specs=[anywhere] * 3,
        out_specs=anywhere,
        scratch_shapes=[
            pltpu.VMEM((2,) + rows, jnp.bfloat16),
            pltpu.VMEM(rows, jnp.bfloat16),
            pltpu.VMEM(rows, jnp.bfloat16),
            pltpu.VMEM((CHUNKS, 2, FRAMES, PLACES, HD), jnp.bfloat16),
            pltpu.VMEM((CHUNKS, FRAMES, PLACES, HD), jnp.bfloat16),
            pltpu.VMEM((3, FRAMES * PLACES, HD), jnp.float32),
            pltpu.VMEM((FRAMES * PLACES, HD), jnp.float32),
            pltpu.VMEM((CHUNKS, FRAMES, PLACES, HD), jnp.bfloat16),
            pltpu.SemaphoreType.REGULAR((FLAT,)),
            sem((3,)),
        ]
        + [sem((CHUNKS,))] * 6,
        compiler_params=pltpu.CompilerParams(
            collective_id=0, has_side_effects=True, vmem_limit_bytes=63 * 1024 * 1024
        ),
        name="two_cores",
    )(query_rows.reshape(rows), key_rows.reshape(rows), value_rows.reshape(rows))
    return result.reshape(shape)


def solution(mesh):
    spec = P(("dp", "ctx"), None, None)
    return jax.shard_map(local, mesh=mesh, in_specs=(spec,) * 3, out_specs=spec, check_vma=False)
```

```python
import functools
import math

import jax
import jax.numpy as jnp
from jax import lax
from jax.experimental import pallas as pl
from jax.experimental.pallas import tpu as pltpu
from jax.sharding import PartitionSpec as P

HEADS = 16
HD = 128
TOK = 256
FRAMES = 64
WIDTH = HEADS * HD
SLOTS = 4
CHUNKS = HEADS // SLOTS
PLACES = 16
MESH = pl.DeviceIdType.MESH
SCALE = HD**-0.5 * math.log2(math.e)
LINE = 8
FLAT = 8
STRIDE = 37
GROUPS = ((1, 4), (3, 5), (2, 7, 6))
LINES = ((4, 3, 5, 2, 6, 1, 7), (1, 7, 2, 6, 3, 5, 4), (3, 5, 1, 7, 4, 2, 6))
FAR_FIRST = sorted(
    range(1, FRAMES),
    key=lambda r: -(min(r // 8, 8 - r // 8) + 4 * (r // 4 % 2) + 0.5 * min(r % 4, 4 - r % 4)),
)


def attend(q, k, v, keep=None):
    scores = lax.dot_general(q, k, (((1,), (1,)), ((), ())), preferred_element_type=jnp.float32)
    if keep is not None:
        scores = jnp.where(keep, scores, -jnp.inf)
    top = jnp.max(scores, axis=1, keepdims=True)
    weights = jnp.exp2((scores - top) * SCALE)
    total = jnp.sum(weights, axis=1, keepdims=True)
    weights = (weights * (1.0 / total)).astype(jnp.bfloat16)
    return jnp.dot(weights, v, preferred_element_type=jnp.float32)


def kernel(q_hbm, k_hbm, v_hbm, o_ref, qk, v, mid, r_qk, r_v, turned, back, o_part, ready, load, s_qk, s_v, s_o, g_qk, g_v, g_o):
    clip, me = lax.axis_index("dp"), lax.axis_index("ctx")
    loads = [
        pltpu.make_async_copy(q_hbm, qk.at[0], load.at[0]),
        pltpu.make_async_copy(k_hbm, qk.at[1], load.at[1]),
        pltpu.make_async_copy(v_hbm, v, load.at[2]),
    ]
    for copy in loads:
        copy.start()

    def at(peer):
        return {"dp": clip, "ctx": peer}

    x, y, z = lax.rem(me, 4), lax.rem(me // 4, 2), me // 8
    turn_x, turn_z = 1 + 2 * lax.rem(clip, 2), 1 + 6 * lax.rem(clip, 2)

    def moved(flat, line):
        new_x = lax.rem(x + lax.rem(flat, 4) * turn_x, 4)
        new_y = lax.rem(y + flat // 4, 2)
        return (lax.rem(z + line * turn_z, LINE) * 2 + new_y) * 4 + new_x

    def every(i):
        r = lax.rem(i * STRIDE, FRAMES)
        return moved(lax.rem(r, FLAT), r // FLAT)

    barrier = pltpu.get_barrier_semaphore()
    for i in range(1, LINE):
        pl.semaphore_signal(barrier, inc=1, device_id=at(moved(0, i)), device_id_type=MESH)
    for i in range(1, FLAT):
        pl.semaphore_signal(barrier, inc=1, device_id=at(moved(i, 0)), device_id_type=MESH)
    pl.semaphore_wait(barrier, LINE + FLAT - 2)
    for i in reversed(range(1, FLAT)):
        back_to_me = (FLAT + 4 - i if i > 4 else 4 - i if i < 4 else 4)
        pl.semaphore_signal(ready.at[back_to_me], inc=1, device_id=at(moved(i, 0)), device_id_type=MESH)

    def block(chunk, peer):
        rows = pl.ds(pl.multiple_of((peer // SLOTS) * PLACES, PLACES), PLACES)
        cols = pl.ds(pl.multiple_of((chunk * SLOTS + lax.rem(peer, SLOTS)) * HD, HD), HD)
        return rows, cols

    def send_qk(chunk, peer):
        rows, cols = block(chunk, peer)
        pltpu.make_async_remote_copy(
            src_ref=qk.at[:, rows, cols], dst_ref=r_qk.at[chunk, :, me],
            send_sem=s_qk.at[chunk], recv_sem=g_qk.at[chunk],
            device_id=at(peer), device_id_type=MESH,
        ).start()

    def send_qk_near(chunk):
        rows, cols = block(chunk, me)
        pltpu.make_async_copy(qk.at[:, rows, cols], r_qk.at[chunk, :, me], g_qk.at[chunk]).start()

        @pl.loop(1, LINE)
        def _(i):
            send_qk(chunk, moved(i, 0))
            send_qk(chunk, moved(0, i))

    def send_qk_lines(flats):
        for flat in flats:
            pl.semaphore_wait(ready.at[flat], 1)

        @pl.loop(0, CHUNKS)
        def _(chunk):
            for i in range(LINE - 1):
                for flat, lines in zip(flats, LINES):
                    send_qk(chunk, moved(flat, lines[i]))

    def send_mid(chunk):
        rows, cols = block(chunk, me)
        pltpu.make_async_copy(mid.at[rows, cols], r_v.at[chunk, me], g_v.at[chunk]).start()

        @pl.loop(1, FRAMES)
        def _(i):
            peer = every(i)
            rows, cols = block(chunk, peer)
            pltpu.make_async_remote_copy(
                src_ref=mid.at[rows, cols], dst_ref=r_v.at[chunk, me],
                send_sem=s_v.at[chunk], recv_sem=g_v.at[chunk],
                device_id=at(peer), device_id_type=MESH,
            ).start()

    def keep_back(chunk):
        rows, cols = block(chunk, me)
        pltpu.make_async_copy(o_part.at[chunk, me], o_ref.at[rows, cols], g_o.at[chunk]).start()

    def send_back(chunk, low, high):
        rows, cols = block(chunk, me)
        for r in FAR_FIRST:
            peer = moved(r % FLAT, r // FLAT)

            @pl.when(jnp.logical_and(peer >= low * FLAT, peer < high * FLAT))
            def _():
                pltpu.make_async_remote_copy(
                    src_ref=o_part.at[chunk, peer], dst_ref=o_ref.at[rows, cols],
                    send_sem=s_o.at[chunk], recv_sem=g_o.at[chunk],
                    device_id=at(peer), device_id_type=MESH,
                ).start()

    def arrived(ref, sem):
        pltpu.make_async_copy(ref, ref, sem).wait()

    def spatial(chunk):
        @pl.loop(0, SLOTS)
        def _(slot):
            cols = pl.ds(pl.multiple_of((chunk * SLOTS + slot) * HD, HD), HD)
            mid[:, cols] = attend(qk[0, :, cols], qk[1, :, cols], v[:, cols]).astype(jnp.bfloat16)

    side = lax.broadcasted_iota(jnp.int32, (2 * FRAMES, 2 * FRAMES), 0) // FRAMES
    other = lax.broadcasted_iota(jnp.int32, (2 * FRAMES, 2 * FRAMES), 1) // FRAMES
    keep = side == other

    def temporal(chunk):
        turned[0] = r_qk[chunk, 0].reshape(FRAMES * PLACES, HD).astype(jnp.float32)
        turned[1] = r_qk[chunk, 1].reshape(FRAMES * PLACES, HD).astype(jnp.float32)
        turned[2] = r_v[chunk].reshape(FRAMES * PLACES, HD).astype(jnp.float32)
        for t in range(0, PLACES, 2):
            trio = [
                jnp.concatenate(
                    [turned[a, pl.ds(t + s, FRAMES, stride=PLACES), :] for s in range(2)], axis=0
                ).astype(jnp.bfloat16)
                for a in range(3)
            ]
            both = attend(*trio, keep)
            back[pl.ds(t, FRAMES, stride=PLACES), :] = both[:FRAMES]
            back[pl.ds(t + 1, FRAMES, stride=PLACES), :] = both[FRAMES:]
        o_part[chunk] = back[...].astype(jnp.bfloat16).reshape(FRAMES, PLACES, HD)

    loads[0].wait()
    loads[1].wait()

    @pl.loop(0, CHUNKS)
    def _(chunk):
        send_qk_near(chunk)

    for flats in GROUPS:
        send_qk_lines(flats)

    loads[2].wait()

    @pl.loop(0, CHUNKS)
    def _(chunk):
        spatial(chunk)
        send_mid(chunk)

    @pl.loop(0, CHUNKS)
    def _(chunk):
        arrived(r_qk.at[chunk], g_qk.at[chunk])
        arrived(r_v.at[chunk], g_v.at[chunk])
        temporal(chunk)
        keep_back(chunk)

        @pl.when(chunk < CHUNKS - 2)
        def _():
            send_back(chunk, 0, LINE)

        @pl.when(chunk >= CHUNKS - 2)
        def _():
            send_back(chunk, 0, 2)

    for chunk in (CHUNKS - 2, CHUNKS - 1):
        send_back(chunk, 2, LINE)

    for chunk in range(CHUNKS):
        cols = pl.ds(chunk * SLOTS * HD, SLOTS * HD)
        arrived(o_ref.at[:, cols], g_o.at[chunk])
    for chunk in range(CHUNKS):
        sent = pl.ds(0, FRAMES - 1)
        arrived(r_qk.at[chunk, :, sent], s_qk.at[chunk])
        arrived(r_v.at[chunk, sent], s_v.at[chunk])
        arrived(o_part.at[chunk, sent], s_o.at[chunk])


def local(query_rows, key_rows, value_rows):
    shape = query_rows.shape
    rows = (TOK, WIDTH)
    anywhere = pl.BlockSpec(memory_space=pl.ANY)
    sem = pltpu.SemaphoreType.DMA
    result = pl.pallas_call(
        kernel,
        out_shape=pltpu.VMEM(rows, jnp.bfloat16),
        in_specs=[anywhere] * 3,
        out_specs=pl.BlockSpec(memory_space=pltpu.VMEM),
        scratch_shapes=[
            pltpu.VMEM((2,) + rows, jnp.bfloat16),
            pltpu.VMEM(rows, jnp.bfloat16),
            pltpu.VMEM(rows, jnp.bfloat16),
            pltpu.VMEM((CHUNKS, 2, FRAMES, PLACES, HD), jnp.bfloat16),
            pltpu.VMEM((CHUNKS, FRAMES, PLACES, HD), jnp.bfloat16),
            pltpu.VMEM((3, FRAMES * PLACES, HD), jnp.float32),
            pltpu.VMEM((FRAMES * PLACES, HD), jnp.float32),
            pltpu.VMEM((CHUNKS, FRAMES, PLACES, HD), jnp.bfloat16),
            pltpu.SemaphoreType.REGULAR((FLAT,)),
            sem((3,)),
        ]
        + [sem((CHUNKS,))] * 6,
        compiler_params=pltpu.CompilerParams(
            collective_id=0, has_side_effects=True, vmem_limit_bytes=62 * 1024 * 1024
        ),
        name="two_cores",
    )(query_rows.reshape(rows), key_rows.reshape(rows), value_rows.reshape(rows))
    return result.reshape(shape)


def solution(mesh):
    spec = P(("dp", "ctx"), None, None)
    return jax.shard_map(local, mesh=mesh, in_specs=(spec,) * 3, out_specs=spec, check_vma=False)
```

```python
import functools
import math

import jax
import jax.numpy as jnp
from jax import lax
from jax.experimental import pallas as pl
from jax.experimental.pallas import tpu as pltpu
from jax.sharding import PartitionSpec as P

HEADS = 16
HD = 128
TOK = 256
FRAMES = 64
WIDTH = HEADS * HD
SLOTS = 4
CHUNKS = HEADS // SLOTS
PLACES = 16
MESH = pl.DeviceIdType.MESH
SCALE = HD**-0.5 * math.log2(math.e)
LINE = 8
FLAT = 8
STRIDE = 37
GROUPS = ((1, 4), (3, 5), (2, 7, 6))
LINES = ((4, 3, 5, 2, 6, 1, 7), (1, 7, 2, 6, 3, 5, 4), (3, 5, 1, 7, 4, 2, 6))
FAR_FIRST = sorted(
    range(1, FRAMES),
    key=lambda r: -(min(r // 8, 8 - r // 8) + 4 * (r // 4 % 2) + 0.5 * min(r % 4, 4 - r % 4)),
)


def weigh(q, k, keep=None):
    scores = lax.dot_general(q, k, (((1,), (1,)), ((), ())), preferred_element_type=jnp.float32)
    if keep is not None:
        scores = jnp.where(keep, scores, -jnp.inf)
    top = jnp.max(scores, axis=1, keepdims=True)
    weights = jnp.exp2((scores - top) * SCALE)
    total = jnp.sum(weights, axis=1, keepdims=True)
    return (weights * (1.0 / total)).astype(jnp.bfloat16)


def attend(q, k, v):
    return jnp.dot(weigh(q, k), v, preferred_element_type=jnp.float32)


def kernel(q_hbm, k_hbm, v_hbm, o_ref, qk, v, mid, r_qk, r_v, turned, shares, back, o_part, ready, load, s_qk, s_v, s_o, g_qk, g_v, g_o):
    clip, me = lax.axis_index("dp"), lax.axis_index("ctx")
    loads = [
        pltpu.make_async_copy(q_hbm, qk.at[0], load.at[0]),
        pltpu.make_async_copy(k_hbm, qk.at[1], load.at[1]),
        pltpu.make_async_copy(v_hbm, v, load.at[2]),
    ]
    for copy in loads:
        copy.start()

    def at(peer):
        return {"dp": clip, "ctx": peer}

    x, y, z = lax.rem(me, 4), lax.rem(me // 4, 2), me // 8
    turn_x, turn_z = 1 + 2 * lax.rem(clip, 2), 1 + 6 * lax.rem(clip, 2)

    def moved(flat, line):
        new_x = lax.rem(x + lax.rem(flat, 4) * turn_x, 4)
        new_y = lax.rem(y + flat // 4, 2)
        return (lax.rem(z + line * turn_z, LINE) * 2 + new_y) * 4 + new_x

    def every(i):
        r = lax.rem(i * STRIDE, FRAMES)
        return moved(lax.rem(r, FLAT), r // FLAT)

    barrier = pltpu.get_barrier_semaphore()
    for i in range(1, LINE):
        pl.semaphore_signal(barrier, inc=1, device_id=at(moved(0, i)), device_id_type=MESH)
    for i in range(1, FLAT):
        pl.semaphore_signal(barrier, inc=1, device_id=at(moved(i, 0)), device_id_type=MESH)
    pl.semaphore_wait(barrier, LINE + FLAT - 2)
    for i in reversed(range(1, FLAT)):
        back_to_me = (FLAT + 4 - i if i > 4 else 4 - i if i < 4 else 4)
        pl.semaphore_signal(ready.at[back_to_me], inc=1, device_id=at(moved(i, 0)), device_id_type=MESH)

    def block(chunk, peer):
        rows = pl.ds(pl.multiple_of((peer // SLOTS) * PLACES, PLACES), PLACES)
        cols = pl.ds(pl.multiple_of((chunk * SLOTS + lax.rem(peer, SLOTS)) * HD, HD), HD)
        return rows, cols

    def send_qk(chunk, peer):
        rows, cols = block(chunk, peer)
        pltpu.make_async_remote_copy(
            src_ref=qk.at[:, rows, cols], dst_ref=r_qk.at[chunk, :, me],
            send_sem=s_qk.at[chunk], recv_sem=g_qk.at[chunk],
            device_id=at(peer), device_id_type=MESH,
        ).start()

    def send_qk_near(chunk):
        rows, cols = block(chunk, me)
        pltpu.make_async_copy(qk.at[:, rows, cols], r_qk.at[chunk, :, me], g_qk.at[chunk]).start()

        @pl.loop(1, LINE)
        def _(i):
            send_qk(chunk, moved(i, 0))
            send_qk(chunk, moved(0, i))

    def send_qk_lines(flats):
        for flat in flats:
            pl.semaphore_wait(ready.at[flat], 1)

        @pl.loop(0, CHUNKS)
        def _(chunk):
            for i in range(LINE - 1):
                for flat, lines in zip(flats, LINES):
                    send_qk(chunk, moved(flat, lines[i]))

    def send_mid(chunk):
        rows, cols = block(chunk, me)
        pltpu.make_async_copy(mid.at[rows, cols], r_v.at[chunk, me], g_v.at[chunk]).start()

        @pl.loop(1, FRAMES)
        def _(i):
            peer = every(i)
            rows, cols = block(chunk, peer)
            pltpu.make_async_remote_copy(
                src_ref=mid.at[rows, cols], dst_ref=r_v.at[chunk, me],
                send_sem=s_v.at[chunk], recv_sem=g_v.at[chunk],
                device_id=at(peer), device_id_type=MESH,
            ).start()

    def keep_back(chunk):
        rows, cols = block(chunk, me)
        pltpu.make_async_copy(o_part.at[chunk, me], o_ref.at[rows, cols], g_o.at[chunk]).start()

    def send_back(chunk, low, high):
        rows, cols = block(chunk, me)
        for r in FAR_FIRST:
            peer = moved(r % FLAT, r // FLAT)

            @pl.when(jnp.logical_and(peer >= low * FLAT, peer < high * FLAT))
            def _():
                pltpu.make_async_remote_copy(
                    src_ref=o_part.at[chunk, peer], dst_ref=o_ref.at[rows, cols],
                    send_sem=s_o.at[chunk], recv_sem=g_o.at[chunk],
                    device_id=at(peer), device_id_type=MESH,
                ).start()

    def arrived(ref, sem):
        pltpu.make_async_copy(ref, ref, sem).wait()

    def spatial(chunk):
        @pl.loop(0, SLOTS)
        def _(slot):
            cols = pl.ds(pl.multiple_of((chunk * SLOTS + slot) * HD, HD), HD)
            mid[:, cols] = attend(qk[0, :, cols], qk[1, :, cols], v[:, cols]).astype(jnp.bfloat16)

    side = lax.broadcasted_iota(jnp.int32, (2 * FRAMES, 2 * FRAMES), 0) // FRAMES
    other = lax.broadcasted_iota(jnp.int32, (2 * FRAMES, 2 * FRAMES), 1) // FRAMES
    keep = side == other

    def turn_two(a, t):
        return jnp.concatenate(
            [turned[a, pl.ds(t + s, FRAMES, stride=PLACES), :] for s in range(2)], axis=0
        ).astype(jnp.bfloat16)

    def temporal_weights(chunk):
        turned[0] = r_qk[chunk, 0].reshape(FRAMES * PLACES, HD).astype(jnp.float32)
        turned[1] = r_qk[chunk, 1].reshape(FRAMES * PLACES, HD).astype(jnp.float32)
        for t in range(0, PLACES, 2):
            shares[chunk, t // 2] = weigh(turn_two(0, t), turn_two(1, t), keep)

    def temporal(chunk):
        turned[2] = r_v[chunk].reshape(FRAMES * PLACES, HD).astype(jnp.float32)
        for t in range(0, PLACES, 2):
            both = jnp.dot(shares[chunk, t // 2], turn_two(2, t), preferred_element_type=jnp.float32)
            back[pl.ds(t, FRAMES, stride=PLACES), :] = both[:FRAMES]
            back[pl.ds(t + 1, FRAMES, stride=PLACES), :] = both[FRAMES:]
        o_part[chunk] = back[...].astype(jnp.bfloat16).reshape(FRAMES, PLACES, HD)

    loads[0].wait()
    loads[1].wait()

    @pl.loop(0, CHUNKS)
    def _(chunk):
        send_qk_near(chunk)

    for flats in GROUPS:
        send_qk_lines(flats)

    loads[2].wait()

    @pl.loop(0, CHUNKS)
    def _(chunk):
        spatial(chunk)
        send_mid(chunk)

    @pl.loop(0, CHUNKS)
    def _(chunk):
        arrived(r_qk.at[chunk], g_qk.at[chunk])
        temporal_weights(chunk)

    @pl.loop(0, CHUNKS)
    def _(chunk):
        arrived(r_v.at[chunk], g_v.at[chunk])
        temporal(chunk)
        keep_back(chunk)

        @pl.when(chunk < CHUNKS - 2)
        def _():
            send_back(chunk, 0, LINE)

        @pl.when(chunk >= CHUNKS - 2)
        def _():
            send_back(chunk, 0, 2)

    for chunk in (CHUNKS - 2, CHUNKS - 1):
        send_back(chunk, 2, LINE)

    for chunk in range(CHUNKS):
        cols = pl.ds(chunk * SLOTS * HD, SLOTS * HD)
        arrived(o_ref.at[:, cols], g_o.at[chunk])
    for chunk in range(CHUNKS):
        sent = pl.ds(0, FRAMES - 1)
        arrived(r_qk.at[chunk, :, sent], s_qk.at[chunk])
        arrived(r_v.at[chunk, sent], s_v.at[chunk])
        arrived(o_part.at[chunk, sent], s_o.at[chunk])


def local(query_rows, key_rows, value_rows):
    shape = query_rows.shape
    rows = (TOK, WIDTH)
    anywhere = pl.BlockSpec(memory_space=pl.ANY)
    sem = pltpu.SemaphoreType.DMA
    result = pl.pallas_call(
        kernel,
        out_shape=pltpu.VMEM(rows, jnp.bfloat16),
        in_specs=[anywhere] * 3,
        out_specs=pl.BlockSpec(memory_space=pltpu.VMEM),
        scratch_shapes=[
            pltpu.VMEM((2,) + rows, jnp.bfloat16),
            pltpu.VMEM(rows, jnp.bfloat16),
            pltpu.VMEM(rows, jnp.bfloat16),
            pltpu.VMEM((CHUNKS, 2, FRAMES, PLACES, HD), jnp.bfloat16),
            pltpu.VMEM((CHUNKS, FRAMES, PLACES, HD), jnp.bfloat16),
            pltpu.VMEM((3, FRAMES * PLACES, HD), jnp.float32),
            pltpu.VMEM((CHUNKS, PLACES // 2, 2 * FRAMES, 2 * FRAMES), jnp.bfloat16),
            pltpu.VMEM((FRAMES * PLACES, HD), jnp.float32),
            pltpu.VMEM((CHUNKS, FRAMES, PLACES, HD), jnp.bfloat16),
            pltpu.SemaphoreType.REGULAR((FLAT,)),
            sem((3,)),
        ]
        + [sem((CHUNKS,))] * 6,
        compiler_params=pltpu.CompilerParams(
            collective_id=0, has_side_effects=True, vmem_limit_bytes=62 * 1024 * 1024
        ),
        name="two_cores",
    )(query_rows.reshape(rows), key_rows.reshape(rows), value_rows.reshape(rows))
    return result.reshape(shape)


def solution(mesh):
    spec = P(("dp", "ctx"), None, None)
    return jax.shard_map(local, mesh=mesh, in_specs=(spec,) * 3, out_specs=spec, check_vma=False)
```
